128 devices in a mesh: row: 16 (over x_hi, y, core), col: 8 (over x_lo, z).
Axes of the slice: x: 4 (x_hi: 2, x_lo: 2; x = x_hi * 2 + x_lo), y: 4, z: 4, core: 2. Of those that a mesh axis runs over, the one named last changes fastest.
Arguments:
- vectors: float32 [131072, 2048], P('row', 'col'), may hold values from -6 to 6
- reflectors: float32 [131072, 512], P('row', 'col'), may hold values from -0.046875 to 0.046875
- tmat: float32 [512, 512], replicated, as said below
- offset: int32 [1], replicated, may hold values from 0 to 32767
- band: int32 [1], replicated, may hold values from 65536 to 98303
Outputs:
- updated: float32 [131072, 2048], P('row', 'col')
The draws below stay inside these ranges and needn't reach their ends.
Inputs may be any that keep to these rules, and one draw needn't show every extreme that they name: tmat is upper triangular with a positive diagonal.
All inputs are finite; a program needn't handle non-finite values.
Results may differ from the reference program's by a relative error of at most 0.000092.
Values sent between devices are 32-bit elements; how exact they have to be, the bound alone decides.
No kernel may reach another device: no remote copies, remote signals or barrier semaphores. Data moves between devices by JAX's collectives and lax.ppermute only.
A program may use at most 128 MiB of HBM per device.

```python
import jax
import jax.numpy as jnp
from jax import lax

N = 131072
NB = 512
TILE = 64
EIGS = 2048
N_ROW = 16


def draw_tmat(key, part):
    key = jax.random.fold_in(key, 11)
    key_diag, key_upper = jax.random.split(key)
    diagonal = jax.random.uniform(key_diag, (NB,), jnp.float32, 1.0, 2.0)
    upper = jax.random.normal(key_upper, (NB, NB), jnp.float32) * (0.5 / NB ** 0.5)
    return jnp.triu(upper, 1) + jnp.diag(diagonal)


def levels(key, shape, cuts, smallest, largest):
    factor_of, own = 1.0, jax.random.fold_in(key, 6)
    for axis_at, shards_of in cuts:
        heights = jnp.exp(jax.random.uniform(jax.random.fold_in(own, axis_at), (shards_of,), jnp.float32, smallest / len(cuts), largest / len(cuts)))
        factor_of = factor_of * jnp.repeat(heights, shape[axis_at] // shards_of).reshape([-1 if axis == axis_at else 1 for axis in range(len(shape))])
    return factor_of


def noise(key, dims, spread, limit, pieces=(), kind=jnp.bfloat16):
    factor_of = levels(key, dims, pieces, -0.22, 0.18) if pieces else 1.0
    result = jax.random.normal(key, dims, jnp.float32) * spread * factor_of
    return jnp.minimum(jnp.maximum(result, -limit), limit).astype(kind)


def setup_inputs(seed: int = 0) -> dict:
    key_list = jax.random.split(jax.random.key(seed), 6)
    return {
        "vectors": noise(key_list[0], (N, EIGS), 1.0, 6.0, ((0, 16), (1, 8)), jnp.float32),
        "reflectors": noise(key_list[1], (N, NB), (N // 8) ** -0.5, 0.046875, ((0, 16), (1, 8)), jnp.float32),
        "tmat": draw_tmat(jax.random.fold_in(key_list[5], 71), 0),
        "offset": jax.random.randint(key_list[3], (1,), 0, N // 4).astype(jnp.int32),
        "band": jax.random.randint(key_list[4], (1,), N // 2, 3 * N // 4).astype(jnp.int32),
    }


def reference(vectors, reflectors, tmat, offset, band):
    row_ids = jnp.arange(N).astype(jnp.int32)[:, None]
    col_ids = jnp.arange(NB).astype(jnp.int32)[None, :]
    first = offset[0] + col_ids
    inside = (row_ids > first) & (row_ids < first + band[0])
    yeff = jnp.where(row_ids == first, jnp.float32(1.0), jnp.where(inside, reflectors, jnp.float32(0.0)))
    products = lax.dot_general(yeff, vectors, (((0,), (0,)), ((), ())), precision=lax.Precision.HIGHEST, preferred_element_type=jnp.float32)
    weights = jnp.dot(tmat, products, precision=lax.Precision.HIGHEST, preferred_element_type=jnp.float32)
    natural = vectors - jnp.dot(yeff, weights, precision=lax.Precision.HIGHEST, preferred_element_type=jnp.float32)
    groups = N // (TILE * N_ROW)
    return natural.reshape(groups, N_ROW, TILE, EIGS).transpose(1, 0, 2, 3).reshape(N, EIGS)
```

```python
import jax
import jax.numpy as jnp
from jax import lax
from jax.experimental import pallas as pl
from jax.experimental.pallas import tpu as pltpu
from jax.sharding import PartitionSpec as P

TILE = 64
BLOCK = 2 * TILE
WINDOW = 50
CHUNKS = 2
YSIZE = 4
ROWS = 16


def row_perm(dx, dy, dc):
    pairs = []
    for x in range(2):
        for y in range(4):
            for c in range(2):
                pairs.append(
                    (x * 8 + y * 2 + c, (x ^ dx) * 8 + ((y + dy) % 4) * 2 + (c ^ dc))
                )
    return pairs


def col_perm(dl, dz):
    return [
        (low * 4 + z, (low ^ dl) * 4 + (z + dz) % 4) for low in range(2) for z in range(4)
    ]


def tile_kernel(y_ref, *out_refs):
    lanes = lax.broadcasted_iota(jnp.int32, (y_ref.shape[0], BLOCK), 1)
    low = lanes < TILE
    rows = y_ref.shape[0] // CHUNKS
    for q in range(8):
        first = y_ref[:, q * BLOCK : (q + 1) * BLOCK]
        second = y_ref[:, 1024 + q * BLOCK : 1024 + (q + 1) * BLOCK]
        even = jnp.where(low, first, pltpu.roll(second, TILE, 1))
        odd = jnp.where(low, pltpu.roll(first, TILE, 1), second)
        for k, out in enumerate(out_refs):
            out[2 * q, 0] = even[k * rows : (k + 1) * rows]
            out[2 * q + 1, 0] = odd[k * rows : (k + 1) * rows]


def cut_tiles(y_t):
    refl, height = y_t.shape
    steps = height // 2048
    rows = refl // CHUNKS
    return pl.pallas_call(
        tile_kernel,
        grid=(steps,),
        in_specs=[pl.BlockSpec((refl, 2048), lambda i: (0, i))],
        out_specs=[pl.BlockSpec((ROWS, 1, rows, BLOCK), lambda i: (0, i, 0, 0))] * CHUNKS,
        out_shape=[jax.ShapeDtypeStruct((ROWS, steps, rows, BLOCK), jnp.float32)] * CHUNKS,
        name="cut_tiles",
    )(y_t)


def per_device(vectors, reflectors, tmat, offset, band):
    height, width = vectors.shape
    position = lax.axis_index("row")
    place = lax.axis_index("col")
    xh, yy, cc = position // 8, (position // 2) % 4, position % 2
    xl, zz = place // 4, place % 4
    w0 = jnp.clip(offset[0] // (BLOCK * ROWS), 0, height // BLOCK - WINDOW)

    view = vectors.reshape(2, 4, 2, 4, 2, TILE, width)
    own = lax.dynamic_index_in_dim(view, xh, 2, keepdims=False)
    other = lax.dynamic_index_in_dim(view, 1 - xh, 2, keepdims=False)
    came_x = [lax.ppermute(other[h], "row", row_perm(1, 0, 0)) for h in range(2)]

    chunks = cut_tiles(reflectors.T)
    blocks = []
    for piece in chunks:
        rows = piece.shape[2]
        cyc = lax.all_to_all(piece, "row", split_axis=0, concat_axis=0, tiled=True)
        cyc = cyc.reshape(height // BLOCK, rows, BLOCK)
        mine = lax.dynamic_slice_in_dim(cyc, w0, WINDOW, 0)
        across = lax.ppermute(mine, "col", col_perm(1, 0))
        pair = jnp.stack([mine, across])
        up = lax.ppermute(pair, "col", col_perm(0, 1))
        down = lax.ppermute(pair, "col", col_perm(0, 3))
        far0 = lax.ppermute(up[0], "col", col_perm(0, 1))
        far1 = lax.ppermute(down[1], "col", col_perm(0, 3))
        far = jnp.stack([far0, far1])
        blocks.append(jnp.stack([pair, down, far, up], axis=1))
    full = jnp.stack(blocks, axis=2)
    nb = 8 * 64
    full = full.transpose(0, 1, 2, 4, 3, 5).reshape(nb, WINDOW * BLOCK)

    cyc_v = jnp.zeros((2, 4, 2, 2, 4, TILE, width), jnp.float32)
    for h in range(2):
        both = jnp.stack([own[h], came_x[h]])
        parts = []
        for dy in range(4):
            send = lax.dynamic_index_in_dim(both, (yy + dy) % 4, 2, keepdims=False)
            parts.append(lax.ppermute(send, "row", row_perm(0, dy, 0)) if dy else send)
        got = jnp.stack(parts)
        keep = lax.dynamic_index_in_dim(got, cc, 3, keepdims=False)
        give = lax.dynamic_index_in_dim(got, 1 - cc, 3, keepdims=False)
        came_c = lax.ppermute(give, "row", row_perm(0, 0, 1))
        for dy in range(4):
            for dx in range(2):
                for dc, source in enumerate((keep, came_c)):
                    cyc_v = lax.dynamic_update_slice(
                        cyc_v,
                        source[dy, dx][None, None, None, None],
                        (xh ^ dx, (yy - dy) % 4, cc ^ dc, h, 0, 0, 0),
                    )
    cyc_v = cyc_v.reshape(height, width)

    span = WINDOW * BLOCK
    stored = w0 * BLOCK + jnp.arange(span, dtype=jnp.int32)
    row_ids = ((stored // TILE) * ROWS + position) * TILE + stored % TILE
    lrel, zrel, inner = jnp.arange(2), jnp.arange(4), jnp.arange(64)
    col_ids = (
        ((lrel ^ xl)[:, None, None] * 4 + ((zrel + zz) % 4)[None, :, None]) * 64 + inner[None, None]
    ).reshape(nb)
    first = (offset[0] + col_ids)[:, None]
    grid = row_ids[None, :]
    inside = (grid > first) & (grid < first + band[0])
    yeff = jnp.where(grid == first, 1.0, jnp.where(inside, full, 0.0))

    active = lax.dynamic_slice_in_dim(cyc_v, w0 * BLOCK, span, 0)
    partial_value = jnp.dot(yeff, active, precision=lax.Precision.HIGH)
    share = lax.all_to_all(
        partial_value.reshape(ROWS, nb // ROWS, width), "row", split_axis=0, concat_axis=0, tiled=True
    ).sum(0)
    products = lax.all_to_all(
        jnp.broadcast_to(share[None], (ROWS, nb // ROWS, width)),
        "row", split_axis=0, concat_axis=0, tiled=True,
    ).reshape(nb, width)
    t_rel = tmat[col_ids][:, col_ids]
    weights = jnp.dot(t_rel, products, precision=lax.Precision.HIGH)
    change = lax.dot_general(
        yeff, weights, (((0,), (0,)), ((), ())), precision=lax.Precision.HIGH
    )
    return lax.dynamic_update_slice_in_dim(cyc_v, active - change, w0 * BLOCK, 0)


def solution(mesh):
    placed = (P("row", "col"), P("row", "col"), P(), P(), P())
    return jax.shard_map(
        per_device, mesh=mesh, in_specs=placed, out_specs=P("row", "col"), check_vma=False
    )
```

```python
import functools

import jax
import jax.numpy as jnp
from jax import lax
from jax.experimental import pallas as pl
from jax.experimental.pallas import tpu as pltpu
from jax.sharding import PartitionSpec as P

TILE = 64
BLOCK = 2 * TILE
WINDOW = 50
SPAN = WINDOW * BLOCK
STEP = 10
ORDER = (0, 1, 3, 2)
CHUNKS = 2
ROWS = 16
F32, BF16 = jnp.float32, jnp.bfloat16


def col_perm(dl, dz):
    return [
        (low * 4 + z, (low ^ dl) * 4 + (z + dz) % 4) for low in range(2) for z in range(4)
    ]


def tile_kernel(y_ref, *out_refs):
    lanes = lax.broadcasted_iota(jnp.int32, (y_ref.shape[0], BLOCK), 1)
    low = lanes < TILE
    rows = y_ref.shape[0] // CHUNKS
    for q in range(8):
        first = y_ref[:, q * BLOCK : (q + 1) * BLOCK]
        second = y_ref[:, 1024 + q * BLOCK : 1024 + (q + 1) * BLOCK]
        even = jnp.where(low, first, pltpu.roll(second, TILE, 1))
        odd = jnp.where(low, pltpu.roll(first, TILE, 1), second)
        for k, out in enumerate(out_refs):
            out[2 * q, 0] = even[k * rows : (k + 1) * rows]
            out[2 * q + 1, 0] = odd[k * rows : (k + 1) * rows]


def cut_tiles(y_t):
    refl, height = y_t.shape
    steps = height // 2048
    rows = refl // CHUNKS
    return pl.pallas_call(
        tile_kernel,
        grid=(steps,),
        in_specs=[pl.BlockSpec((refl, 2048), lambda i: (0, i))],
        out_specs=[pl.BlockSpec((ROWS, 1, rows, BLOCK), lambda i: (0, i, 0, 0))] * CHUNKS,
        out_shape=[jax.ShapeDtypeStruct((ROWS, steps, rows, BLOCK), F32)] * CHUNKS,
        name="cut_tiles",
    )(y_t)


def split(value):
    high = value.astype(BF16)
    return high, (value - high.astype(F32)).astype(BF16)


def window_rows(width, lane=0):
    return pl.BlockSpec(
        (pl.Element(STEP * BLOCK), pl.Element(width)),
        lambda i, s: (pl.multiple_of((s[0] + i * STEP) * BLOCK, BLOCK), lane),
    )


def prepare_kernel(info, *refs):
    chunk_refs, (high, low, high_t, low_t) = refs[: 2 * CHUNKS], refs[-4:]
    rows = chunk_refs[0].shape[2]
    step = pl.program_id(0)
    lane = lax.broadcasted_iota(jnp.int32, (rows, BLOCK), 1)
    spread = (lane // TILE) * (ROWS * TILE) + lane % TILE
    spread = spread - lax.broadcasted_iota(jnp.int32, (rows, BLOCK), 0)
    band = info[3]
    for w in range(STEP):
        start = (info[0] + step * STEP + w) * (BLOCK * ROWS) + info[1] * TILE - info[2]
        parts = []
        for half in range(2):
            for k in range(CHUNKS):
                raw = chunk_refs[2 * k + half][0, w]
                away = spread + (start - info[4 + half] - k * rows)
                kept = jnp.where((away > 0) & (away < band), raw, 0.0)
                parts.append(jnp.where(away == 0, 1.0, kept))
        value = jnp.concatenate(parts, axis=0)
        at = slice(w * BLOCK, (w + 1) * BLOCK)
        high[:, at], low[:, at] = split(value)
        high_t[at, :], low_t[at, :] = split(value.T)


def prepare(info, chunks, place, height, count, before):
    specs, arrays = [], []
    for halves in chunks:
        for array, lead in halves:
            rows = array.shape[2]
            specs.append(
                pl.BlockSpec((1, STEP, rows, BLOCK), functools.partial(lambda lead, i, s: (lead, i, 0, 0), lead))
            )
            arrays.append(array)
    aliases = {1 + len(arrays) + k: k for k in range(len(before))}
    specs += [pl.BlockSpec(memory_space=pl.ANY)] * len(before)
    wide = jax.ShapeDtypeStruct((count, SPAN), BF16)
    tall = jax.ShapeDtypeStruct((height, count), BF16)
    wide_spec = pl.BlockSpec((BLOCK, STEP * BLOCK), lambda i, s: (place, i))
    tall_spec = window_rows(BLOCK, place * BLOCK)
    return pl.pallas_call(
        prepare_kernel,
        grid_spec=pltpu.PrefetchScalarGridSpec(
            num_scalar_prefetch=1,
            grid=(WINDOW // STEP,),
            in_specs=specs,
            out_specs=[wide_spec, wide_spec, tall_spec, tall_spec],
        ),
        out_shape=[wide, wide, tall, tall],
        input_output_aliases=aliases,
        name="prepare",
        cost_estimate=pl.CostEstimate(flops=10**9, bytes_accessed=2 * 10**7, transcendentals=0),
    )(info, *arrays, *before)


def dot(a, b):
    return jnp.dot(a, b, preferred_element_type=F32)


def project_kernel(info, v_ref, high_ref, low_ref, out):
    @pl.when(pl.program_id(0) == 0)
    def _():
        out[...] = jnp.zeros_like(out)

    v_high, v_low = split(v_ref[...])
    high = high_ref[...]
    out[...] += dot(high, v_high) + dot(low_ref[...], v_high) + dot(high, v_low)


def project(info, cyc_v, high, low, start, count):
    width = cyc_v.shape[1]
    wide = pl.BlockSpec((count, STEP * BLOCK), lambda i, s: (start // count, i))
    return pl.pallas_call(
        project_kernel,
        grid_spec=pltpu.PrefetchScalarGridSpec(
            num_scalar_prefetch=1,
            grid=(WINDOW // STEP,),
            in_specs=[window_rows(width), wide, wide],
            out_specs=pl.BlockSpec((count, width), lambda i, s: (0, 0)),
        ),
        out_shape=jax.ShapeDtypeStruct((count, width), F32),
        name="project",
        cost_estimate=pl.CostEstimate(flops=6 * count * SPAN * 256, bytes_accessed=2 * 10**7, transcendentals=0),
    )(info, cyc_v, high, low)


def apply_kernel(info, v_ref, t_ref, p_ref, high_ref, low_ref, out, w_high, w_low):
    step = pl.program_id(0)
    rows = v_ref.shape[0]

    @pl.when(step == 0)
    def _():
        t_high, t_low = split(t_ref[...])
        p_high, p_low = split(p_ref[...])
        weights = dot(t_high, p_high) + dot(t_low, p_high) + dot(t_high, p_low)
        w_high[...], w_low[...] = split(weights)

    start = info[0] * BLOCK - step * rows
    touched = (start < rows) & (start + SPAN > 0)

    @pl.when(touched)
    def _():
        high = high_ref[...]
        change = dot(high, w_high[...]) + dot(low_ref[...], w_high[...]) + dot(high, w_low[...])
        at = lax.broadcasted_iota(jnp.int32, change.shape, 0) - start
        value = v_ref[...]
        out[...] = jnp.where((at >= 0) & (at < SPAN), value - change, value)

    @pl.when(jnp.logical_not(touched))
    def _():
        out[...] = v_ref[...]


def apply(info, cyc_v, t_rel, products, high, low):
    nb, (height, width) = high.shape[1], cyc_v.shape
    rows = 8 * BLOCK
    tall = pl.BlockSpec((rows, nb), lambda i, s: (i, 0))
    plain = pl.BlockSpec((rows, width), lambda i, s: (i, 0))
    return pl.pallas_call(
        apply_kernel,
        grid_spec=pltpu.PrefetchScalarGridSpec(
            num_scalar_prefetch=1,
            grid=(height // rows,),
            in_specs=[
                plain,
                pl.BlockSpec((nb, nb), lambda i, s: (0, 0)),
                pl.BlockSpec((nb, width), lambda i, s: (0, 0)),
            ]
            + [tall] * 2,
            out_specs=plain,
            scratch_shapes=[pltpu.VMEM((nb, width), BF16)] * 2,
        ),
        out_shape=jax.ShapeDtypeStruct(cyc_v.shape, F32),
        name="apply",
        cost_estimate=pl.CostEstimate(flops=6 * 512 * SPAN * 256, bytes_accessed=3 * 10**7, transcendentals=0),
    )(info, cyc_v, t_rel, products, high, low)


def per_device(vectors, reflectors, tmat, offset, band):
    height, width = vectors.shape
    refl = reflectors.shape[1]
    nb = 8 * refl
    position = lax.axis_index("row")
    place = lax.axis_index("col")
    xl, zz = place // 4, place % 4
    w0 = jnp.clip(offset[0] // (BLOCK * ROWS), 0, height // BLOCK - WINDOW)

    pieces = [
        lax.all_to_all(piece, "row", split_axis=0, concat_axis=0, tiled=True)
        for piece in cut_tiles(reflectors.T)
    ]
    pairs = []
    for piece in pieces:
        rows = piece.shape[2]
        cyc = piece.reshape(height // BLOCK, rows, BLOCK)
        mine = lax.dynamic_slice_in_dim(cyc, w0, WINDOW, 0)
        across = lax.ppermute(mine, "col", col_perm(1, 0))
        pairs.append(jnp.stack([mine, across]))

    source = vectors.reshape(height // (ROWS * TILE), ROWS, TILE, width).transpose(1, 0, 2, 3)
    source, *_ = lax.optimization_barrier((source, *pairs))
    cyc_v = lax.all_to_all(source, "row", split_axis=0, concat_axis=0, tiled=True).reshape(height, width)

    groups = [[], [], [], []]
    for pair in pairs:
        up = lax.ppermute(pair, "col", col_perm(0, 1))
        down = lax.ppermute(pair, "col", col_perm(0, 3))
        far0 = lax.ppermute(up[:1], "col", col_perm(0, 1))
        far1 = lax.ppermute(down[1:], "col", col_perm(0, 3))
        groups[0].append(((pair, 0), (pair, 1)))
        groups[1].append(((down, 0), (down, 1)))
        groups[2].append(((far0, 0), (far1, 0)))
        groups[3].append(((up, 0), (up, 1)))

    ready = ()
    ids = []
    for n, g in enumerate(ORDER):
        base = ((zz + g) % 4) * refl
        starts = [(xl ^ half) * 4 * refl + base for half in range(2)]
        info = jnp.stack([w0, position, offset[0], band[0], *starts]).astype(jnp.int32)
        ready = prepare(info, groups[g], n, height, nb, ready)
        ids += [start + jnp.arange(refl) for start in starts]
    ids = jnp.concatenate(ids)
    high, low, high_t, low_t = ready

    info = w0[None].astype(jnp.int32)
    partial_value = project(info, cyc_v, high, low, 0, nb)
    share = lax.all_to_all(
        partial_value.reshape(ROWS, nb // ROWS, width), "row", split_axis=0, concat_axis=0, tiled=True
    ).sum(0)
    products = lax.all_to_all(
        jnp.broadcast_to(share[None], (ROWS, nb // ROWS, width)),
        "row", split_axis=0, concat_axis=0, tiled=True,
    ).reshape(nb, width)
    t_rel = tmat[ids][:, ids]
    return apply(info, cyc_v, t_rel, products, high_t, low_t)


def solution(mesh):
    placed = (P("row", "col"), P("row", "col"), P(), P(), P())
    return jax.shard_map(
        per_device, mesh=mesh, in_specs=placed, out_specs=P("row", "col"), check_vma=False
    )
```

```python
import functools

import jax
import jax.numpy as jnp
from jax import lax
from jax.experimental import pallas as pl
from jax.experimental.pallas import tpu as pltpu
from jax.sharding import PartitionSpec as P

TILE = 64
BLOCK = 2 * TILE
WINDOW = 50
SPAN = WINDOW * BLOCK
STEP = 5
PARTS = (25, 25)
ORDER = (0, 1, 3, 2)
ROWS = 16
F32, BF16 = jnp.float32, jnp.bfloat16
PARAMS = pltpu.CompilerParams(vmem_limit_bytes=60 * 2**20)


def col_perm(dl, dz):
    return [
        (low * 4 + z, (low ^ dl) * 4 + (z + dz) % 4) for low in range(2) for z in range(4)
    ]


def tile_kernel(y_ref, out_ref):
    lanes = lax.broadcasted_iota(jnp.int32, (y_ref.shape[0], BLOCK), 1)
    low = lanes < TILE
    for q in range(8):
        first = y_ref[:, q * BLOCK : (q + 1) * BLOCK]
        second = y_ref[:, 1024 + q * BLOCK : 1024 + (q + 1) * BLOCK]
        out_ref[2 * q, 0] = jnp.where(low, first, pltpu.roll(second, TILE, 1))
        out_ref[2 * q + 1, 0] = jnp.where(low, pltpu.roll(first, TILE, 1), second)


def cut_tiles(y_t):
    refl, height = y_t.shape
    steps = height // 2048
    return pl.pallas_call(
        tile_kernel,
        grid=(steps,),
        in_specs=[pl.BlockSpec((refl, 2048), lambda i: (0, i))],
        out_specs=pl.BlockSpec((ROWS, 1, refl, BLOCK), lambda i: (0, i, 0, 0)),
        out_shape=jax.ShapeDtypeStruct((ROWS, steps, refl, BLOCK), F32),
        name="cut_tiles",
        compiler_params=PARAMS,
    )(y_t)


def split(value):
    high = value.astype(BF16)
    return high, (value - high.astype(F32)).astype(BF16)


def prepare_kernel(skip, info, *refs):
    halves, (high, low, high_t, low_t, done) = refs[:2], refs[-5:]
    done[...] = jnp.zeros_like(done)
    rows = halves[0].shape[2]
    step = pl.program_id(0)
    lane = lax.broadcasted_iota(jnp.int32, (rows, BLOCK), 1)
    spread = (lane // TILE) * (ROWS * TILE) + lane % TILE
    spread = spread - lax.broadcasted_iota(jnp.int32, (rows, BLOCK), 0)
    band = info[3]
    for w in range(STEP):
        start = (info[0] + skip + step * STEP + w) * (BLOCK * ROWS) + info[1] * TILE - info[2]
        parts = []
        for half in range(2):
            away = spread + (start - info[4 + half])
            kept = jnp.where((away > 0) & (away < band), halves[half][0, w], 0.0)
            parts.append(jnp.where(away == 0, 1.0, kept))
        value = jnp.concatenate(parts, axis=0)
        at = slice(w * BLOCK, (w + 1) * BLOCK)
        high[:, at], low[:, at] = split(value)
        high_t[0, at, :], low_t[0, at, :] = split(value.T)


def prepare(info, halves, place, skip, height, count, before):
    arrays = [array for array, _ in halves]
    blocks, rows = arrays[0].shape[1:3]
    specs = [
        pl.BlockSpec((1, STEP, rows, BLOCK), functools.partial(lambda lead, i, s: (lead, i, 0, 0), lead))
        for _, lead in halves
    ]
    aliases = {3 + k: k for k in range(len(before))}
    specs += [pl.BlockSpec(memory_space=pl.ANY)] * len(before)
    wide = jax.ShapeDtypeStruct((count, SPAN), BF16)
    tall = jax.ShapeDtypeStruct((count // BLOCK, height, BLOCK), BF16)
    wide_spec = pl.BlockSpec((BLOCK, STEP * BLOCK), lambda i, s: (place, i + skip // STEP))
    tall_spec = pl.BlockSpec(
        (pl.Element(1), pl.Element(STEP * BLOCK), pl.Element(BLOCK)),
        lambda i, s: (place, pl.multiple_of((s[0] + skip + i * STEP) * BLOCK, BLOCK), 0),
    )
    done = jax.ShapeDtypeStruct((8, BLOCK), F32)
    done_spec = pl.BlockSpec((8, BLOCK), lambda i, s: (0, 0))
    return pl.pallas_call(
        functools.partial(prepare_kernel, skip),
        grid_spec=pltpu.PrefetchScalarGridSpec(
            num_scalar_prefetch=1,
            grid=(blocks // STEP,),
            in_specs=specs,
            out_specs=[wide_spec, wide_spec, tall_spec, tall_spec, done_spec],
        ),
        out_shape=[wide, wide, tall, tall, done],
        input_output_aliases=aliases,
        name="prepare",
        compiler_params=PARAMS,
        cost_estimate=pl.CostEstimate(flops=10**9, bytes_accessed=10**7, transcendentals=0),
    )(info, *arrays, *before)


def dot(a, b):
    return jnp.dot(a, b, preferred_element_type=F32)


def project_kernel(info, v_ref, high_ref, low_ref, out):
    @pl.when(pl.program_id(0) == 0)
    def _():
        out[...] = jnp.zeros_like(out)

    v_high, v_low = split(v_ref[...])
    high = high_ref[...]
    out[...] += dot(high, v_high) + dot(low_ref[...], v_high) + dot(high, v_low)


def project(info, cyc_v, high, low):
    width, count = cyc_v.shape[1], high.shape[0]
    rows = 2 * STEP * BLOCK
    wide = pl.BlockSpec((count, rows), lambda i, s: (0, i))
    window = pl.BlockSpec(
        (pl.Element(rows), pl.Element(width)),
        lambda i, s: (pl.multiple_of(s[0] * BLOCK + i * rows, BLOCK), 0),
    )
    return pl.pallas_call(
        project_kernel,
        grid_spec=pltpu.PrefetchScalarGridSpec(
            num_scalar_prefetch=1,
            grid=(SPAN // rows,),
            in_specs=[window, wide, wide],
            out_specs=pl.BlockSpec((count, width), lambda i, s: (0, 0)),
        ),
        out_shape=jax.ShapeDtypeStruct((count, width), F32),
        name="project",
        compiler_params=PARAMS,
        cost_estimate=pl.CostEstimate(flops=6 * count * SPAN * width, bytes_accessed=2 * 10**7, transcendentals=0),
    )(info, cyc_v, high, low)


def apply_kernel(info, v_ref, t_ref, p_ref, high_ref, low_ref, out, w_high, w_low):
    step = pl.program_id(0)
    rows = v_ref.shape[0]

    @pl.when(step == 0)
    def _():
        t_high, t_low = split(t_ref[...])
        p_high, p_low = split(p_ref[...])
        weights = dot(t_high, p_high) + dot(t_low, p_high) + dot(t_high, p_low)
        w_high[...], w_low[...] = split(weights)

    start = info[0] * BLOCK - step * rows
    touched = (start < rows) & (start + SPAN > 0)

    @pl.when(touched)
    def _():
        high = jnp.concatenate([high_ref[g] for g in range(4)], axis=1)
        low = jnp.concatenate([low_ref[g] for g in range(4)], axis=1)
        change = dot(high, w_high[...]) + dot(low, w_high[...]) + dot(high, w_low[...])
        at = lax.broadcasted_iota(jnp.int32, change.shape, 0) - start
        value = v_ref[...]
        out[...] = jnp.where((at >= 0) & (at < SPAN), value - change, value)

    @pl.when(jnp.logical_not(touched))
    def _():
        out[...] = v_ref[...]


def apply(info, cyc_v, t_rel, products, high, low):
    nb, (height, width) = high.shape[0] * BLOCK, cyc_v.shape
    rows = 8 * BLOCK
    tall = pl.BlockSpec((nb // BLOCK, rows, BLOCK), lambda i, s: (0, i, 0))
    plain = pl.BlockSpec((rows, width), lambda i, s: (i, 0))
    return pl.pallas_call(
        apply_kernel,
        grid_spec=pltpu.PrefetchScalarGridSpec(
            num_scalar_prefetch=1,
            grid=(height // rows,),
            in_specs=[
                plain,
                pl.BlockSpec((nb, nb), lambda i, s: (0, 0)),
                pl.BlockSpec((nb, width), lambda i, s: (0, 0)),
            ]
            + [tall] * 2,
            out_specs=plain,
            scratch_shapes=[pltpu.VMEM((nb, width), BF16)] * 2,
        ),
        out_shape=jax.ShapeDtypeStruct(cyc_v.shape, F32),
        name="apply",
        compiler_params=PARAMS,
        cost_estimate=pl.CostEstimate(flops=6 * 512 * SPAN * 256, bytes_accessed=3 * 10**7, transcendentals=0),
    )(info, cyc_v, t_rel, products, high, low)


def row_perm(dx, dy, dc):
    return [
        (x * 8 + y * 2 + c, (x ^ dx) * 8 + ((y + dy) % 4) * 2 + (c ^ dc))
        for x in range(2)
        for y in range(4)
        for c in range(2)
    ]


def sum_over_rows(value, position):
    core_perm, x_perm = row_perm(0, 0, 1), row_perm(1, 0, 0)
    cc, xh = position % 2, position // 8

    def halve(value, bit, perm):
        n = value.shape[0] // 2
        keep = lax.dynamic_slice_in_dim(value, bit * n, n, 0)
        give = lax.dynamic_slice_in_dim(value, (1 - bit) * n, n, 0)
        return keep + lax.ppermute(give, "row", perm)

    def join(value, bit, perm):
        other = lax.ppermute(value, "row", perm)
        first, second = jnp.where(bit == 0, value, other), jnp.where(bit == 0, other, value)
        return jnp.concatenate([first, second])

    value = halve(halve(value, cc, core_perm), xh, x_perm)
    value = value + sum(lax.ppermute(value, "row", row_perm(0, dy, 0)) for dy in (1, 2, 3))
    return join(join(value, xh, x_perm), cc, core_perm)


def per_device(vectors, reflectors, tmat, offset, band):
    height, width = vectors.shape
    refl = reflectors.shape[1]
    nb = 8 * refl
    position = lax.axis_index("row")
    place = lax.axis_index("col")
    xl, zz = place // 4, place % 4
    w0 = jnp.clip(offset[0] // (BLOCK * ROWS), 0, height // BLOCK - WINDOW)

    cut = lax.all_to_all(cut_tiles(reflectors.T), "row", split_axis=0, concat_axis=0, tiled=True)
    cut = cut.reshape(height // BLOCK, refl, BLOCK)
    skips = [sum(PARTS[:k]) for k in range(len(PARTS))]
    mine = lax.dynamic_slice_in_dim(cut, w0, WINDOW, 0)
    across = lax.ppermute(mine, "col", col_perm(1, 0))
    pairs = [jnp.stack([mine[k : k + n], across[k : k + n]]) for k, n in zip(skips, PARTS)]

    source = vectors.reshape(height // (ROWS * TILE), ROWS, TILE, width).transpose(1, 0, 2, 3)
    source, _ = lax.optimization_barrier((source, across))
    cyc_v = lax.all_to_all(source, "row", split_axis=0, concat_axis=0, tiled=True).reshape(height, width)

    infos, ids = {}, []
    for g in ORDER:
        base = ((zz + g) % 4) * refl
        starts = [(xl ^ half) * 4 * refl + base for half in range(2)]
        infos[g] = jnp.stack([w0, position, offset[0], band[0], *starts]).astype(jnp.int32)
        ids += [start + jnp.arange(refl) for start in starts]
    ids = jnp.concatenate(ids)
    t_rel = tmat[ids][:, ids]
    infos[0] = infos[0] + (t_rel[0, 0] * 0.0).astype(jnp.int32)

    ready = ()

    def arrive(k, g, halves):
        nonlocal ready
        *ready, done = prepare(infos[g], halves, ORDER.index(g), skips[k], height, nb, ready)
        return done

    def forward(up, down, done):
        zero = sum(token[0, 0] for token in done)
        far0 = lax.ppermute(up[:1] + zero, "col", col_perm(0, 1))
        far1 = lax.ppermute(down[1:] + zero, "col", col_perm(0, 3))
        return (far0, 0), (far1, 0)

    both = [
        (lax.ppermute(pair, "col", col_perm(0, 1)), lax.ppermute(pair, "col", col_perm(0, 3)))
        for pair in pairs
    ]
    done = [arrive(k, 0, ((pair, 0), (pair, 1))) for k, pair in enumerate(pairs)]
    fars = []
    for k, (up, down) in enumerate(both):
        fars.append(forward(up, down, done))
        done = [arrive(k, 1, ((down, 0), (down, 1))), arrive(k, 3, ((up, 0), (up, 1)))]
    info = w0[None].astype(jnp.int32)
    for k in range(len(PARTS)):
        arrive(k, 2, fars[k])
    high, low, high_t, low_t = ready
    partial_value = project(info, cyc_v, high, low)
    products = sum_over_rows(partial_value, position)
    return apply(info, cyc_v, t_rel, products, high_t, low_t)


def solution(mesh):
    placed = (P("row", "col"), P("row", "col"), P(), P(), P())
    return jax.shard_map(
        per_device, mesh=mesh, in_specs=placed, out_specs=P("row", "col"), check_vma=False
    )
```

```python
import functools

import jax
import jax.numpy as jnp
from jax import lax
from jax.experimental import pallas as pl
from jax.experimental.pallas import tpu as pltpu
from jax.sharding import PartitionSpec as P

TILE = 64
BLOCK = 2 * TILE
WINDOW = 50
SPAN = WINDOW * BLOCK
STEP = 5
PARTS = (30, 20)
ORDER = (0, 1, 3, 2)
ROWS = 16
F32, BF16 = jnp.float32, jnp.bfloat16
PARAMS = pltpu.CompilerParams(vmem_limit_bytes=60 * 2**20)


def col_perm(dl, dz):
    return [
        (low * 4 + z, (low ^ dl) * 4 + (z + dz) % 4) for low in range(2) for z in range(4)
    ]


def tile_kernel(y_ref, out_ref):
    lanes = lax.broadcasted_iota(jnp.int32, (y_ref.shape[0], BLOCK), 1)
    low = lanes < TILE
    for q in range(8):
        first = y_ref[:, q * BLOCK : (q + 1) * BLOCK]
        second = y_ref[:, 1024 + q * BLOCK : 1024 + (q + 1) * BLOCK]
        out_ref[2 * q, 0] = jnp.where(low, first, pltpu.roll(second, TILE, 1))
        out_ref[2 * q + 1, 0] = jnp.where(low, pltpu.roll(first, TILE, 1), second)


def cut_tiles(y_t):
    refl, height = y_t.shape
    steps = height // 2048
    return pl.pallas_call(
        tile_kernel,
        grid=(steps,),
        in_specs=[pl.BlockSpec((refl, 2048), lambda i: (0, i))],
        out_specs=pl.BlockSpec((ROWS, 1, refl, BLOCK), lambda i: (0, i, 0, 0)),
        out_shape=jax.ShapeDtypeStruct((ROWS, steps, refl, BLOCK), F32),
        name="cut_tiles",
        compiler_params=PARAMS,
    )(y_t)


def split(value):
    high = value.astype(BF16)
    return high, (value - high.astype(F32)).astype(BF16)


def prepare_kernel(skip, info, *refs):
    halves, (high, low, high_t, low_t, done) = refs[:2], refs[-5:]
    done[...] = jnp.zeros_like(done)
    rows = halves[0].shape[2]
    step = pl.program_id(0)
    lane = lax.broadcasted_iota(jnp.int32, (rows, BLOCK), 1)
    spread = (lane // TILE) * (ROWS * TILE) + lane % TILE
    spread = spread - lax.broadcasted_iota(jnp.int32, (rows, BLOCK), 0)
    band = info[3]
    for w in range(STEP):
        start = (info[0] + skip + step * STEP + w) * (BLOCK * ROWS) + info[1] * TILE - info[2]
        parts = []
        for half in range(2):
            away = spread + (start - info[4 + half])
            kept = jnp.where((away > 0) & (away < band), halves[half][0, w], 0.0)
            parts.append(jnp.where(away == 0, 1.0, kept))
        value = jnp.concatenate(parts, axis=0)
        at = slice(w * BLOCK, (w + 1) * BLOCK)
        high[:, at], low[:, at] = split(value)
        high_t[0, at, :], low_t[0, at, :] = split(value.T)


def prepare(info, halves, place, skip, height, count, before):
    arrays = [array for array, _ in halves]
    blocks, rows = arrays[0].shape[1:3]
    specs = [
        pl.BlockSpec((1, STEP, rows, BLOCK), functools.partial(lambda lead, i, s: (lead, i, 0, 0), lead))
        for _, lead in halves
    ]
    aliases = {3 + k: k for k in range(len(before))}
    specs += [pl.BlockSpec(memory_space=pl.ANY)] * len(before)
    wide = jax.ShapeDtypeStruct((count, SPAN), BF16)
    tall = jax.ShapeDtypeStruct((count // BLOCK, height, BLOCK), BF16)
    wide_spec = pl.BlockSpec((BLOCK, STEP * BLOCK), lambda i, s: (place, i + skip // STEP))
    tall_spec = pl.BlockSpec(
        (pl.Element(1), pl.Element(STEP * BLOCK), pl.Element(BLOCK)),
        lambda i, s: (place, pl.multiple_of((s[0] + skip + i * STEP) * BLOCK, BLOCK), 0),
    )
    done = jax.ShapeDtypeStruct((8, BLOCK), F32)
    done_spec = pl.BlockSpec((8, BLOCK), lambda i, s: (0, 0))
    return pl.pallas_call(
        functools.partial(prepare_kernel, skip),
        grid_spec=pltpu.PrefetchScalarGridSpec(
            num_scalar_prefetch=1,
            grid=(blocks // STEP,),
            in_specs=specs,
            out_specs=[wide_spec, wide_spec, tall_spec, tall_spec, done_spec],
        ),
        out_shape=[wide, wide, tall, tall, done],
        input_output_aliases=aliases,
        name="prepare",
        compiler_params=PARAMS,
        cost_estimate=pl.CostEstimate(flops=10**9, bytes_accessed=10**7, transcendentals=0),
    )(info, *arrays, *before)


def dot(a, b):
    return jnp.dot(a, b, preferred_element_type=F32)


def project_kernel(info, v_ref, high_ref, low_ref, out):
    @pl.when(pl.program_id(0) == 0)
    def _():
        out[...] = jnp.zeros_like(out)

    v_high, v_low = split(v_ref[...])
    high = high_ref[...]
    left = jnp.concatenate([high, low_ref[...], high], axis=1)
    out[...] += dot(left, jnp.concatenate([v_high, v_high, v_low], axis=0))


def project(info, cyc_v, high, low):
    width, count = cyc_v.shape[1], high.shape[0]
    rows = 2 * STEP * BLOCK
    wide = pl.BlockSpec((count, rows), lambda i, s: (0, i))
    window = pl.BlockSpec(
        (pl.Element(rows), pl.Element(width)),
        lambda i, s: (pl.multiple_of(s[0] * BLOCK + i * rows, BLOCK), 0),
    )
    return pl.pallas_call(
        project_kernel,
        grid_spec=pltpu.PrefetchScalarGridSpec(
            num_scalar_prefetch=1,
            grid=(SPAN // rows,),
            in_specs=[window, wide, wide],
            out_specs=pl.BlockSpec((count, width), lambda i, s: (0, 0)),
        ),
        out_shape=jax.ShapeDtypeStruct((count, width), F32),
        name="project",
        compiler_params=PARAMS,
        cost_estimate=pl.CostEstimate(flops=6 * count * SPAN * width, bytes_accessed=2 * 10**7, transcendentals=0),
    )(info, cyc_v, high, low)


def apply_kernel(info, v_ref, t_ref, p_ref, high_ref, low_ref, out, w_all):
    step = pl.program_id(0)
    rows = v_ref.shape[0]

    @pl.when(step == 0)
    def _():
        t_high, t_low = split(t_ref[...])
        p_high, p_low = split(p_ref[...])
        weights = dot(t_high, p_high) + dot(t_low, p_high) + dot(t_high, p_low)
        w_high, w_low = split(weights)
        w_all[...] = jnp.concatenate([w_high, w_high, w_low], axis=0)

    start = info[0] * BLOCK - step * rows
    touched = (start < rows) & (start + SPAN > 0)

    @pl.when(touched)
    def _():
        high = [high_ref[g] for g in range(4)]
        low = [low_ref[g] for g in range(4)]
        change = dot(jnp.concatenate(high + low + high, axis=1), w_all[...])
        at = lax.broadcasted_iota(jnp.int32, change.shape, 0) - start
        value = v_ref[...]
        out[...] = jnp.where((at >= 0) & (at < SPAN), value - change, value)

    @pl.when(jnp.logical_not(touched))
    def _():
        out[...] = v_ref[...]


def apply(info, cyc_v, t_rel, products, high, low):
    nb, (height, width) = high.shape[0] * BLOCK, cyc_v.shape
    rows = 8 * BLOCK
    held = lambda i, s: jnp.clip(i, s[0] * BLOCK // rows, (s[0] * BLOCK + SPAN - 1) // rows)
    tall = pl.BlockSpec((nb // BLOCK, rows, BLOCK), lambda i, s: (0, held(i, s), 0))
    plain = pl.BlockSpec((rows, width), lambda i, s: (i, 0))
    return pl.pallas_call(
        apply_kernel,
        grid_spec=pltpu.PrefetchScalarGridSpec(
            num_scalar_prefetch=1,
            grid=(height // rows,),
            in_specs=[
                plain,
                pl.BlockSpec((nb, nb), lambda i, s: (0, 0)),
                pl.BlockSpec((nb, width), lambda i, s: (0, 0)),
            ]
            + [tall] * 2,
            out_specs=plain,
            scratch_shapes=[pltpu.VMEM((3 * nb, width), BF16)],
        ),
        out_shape=jax.ShapeDtypeStruct(cyc_v.shape, F32),
        name="apply",
        compiler_params=PARAMS,
        cost_estimate=pl.CostEstimate(flops=6 * 512 * SPAN * 256, bytes_accessed=3 * 10**7, transcendentals=0),
    )(info, cyc_v, t_rel, products, high, low)


def row_perm(dx, dy, dc):
    return [
        (x * 8 + y * 2 + c, (x ^ dx) * 8 + ((y + dy) % 4) * 2 + (c ^ dc))
        for x in range(2)
        for y in range(4)
        for c in range(2)
    ]


def sum_over_rows(value, position):
    core_perm, x_perm = row_perm(0, 0, 1), row_perm(1, 0, 0)
    cc, xh = position % 2, position // 8

    def halve(value, bit, perm):
        n = value.shape[0] // 2
        keep = lax.dynamic_slice_in_dim(value, bit * n, n, 0)
        give = lax.dynamic_slice_in_dim(value, (1 - bit) * n, n, 0)
        return keep + lax.ppermute(give, "row", perm)

    def join(value, bit, perm):
        other = lax.ppermute(value, "row", perm)
        first, second = jnp.where(bit == 0, value, other), jnp.where(bit == 0, other, value)
        return jnp.concatenate([first, second])

    value = halve(halve(value, cc, core_perm), xh, x_perm)
    value = value + sum(lax.ppermute(value, "row", row_perm(0, dy, 0)) for dy in (1, 2, 3))
    return join(join(value, xh, x_perm), cc, core_perm)


def per_device(vectors, reflectors, tmat, offset, band):
    height, width = vectors.shape
    refl = reflectors.shape[1]
    nb = 8 * refl
    position = lax.axis_index("row")
    place = lax.axis_index("col")
    xl, zz = place // 4, place % 4
    w0 = jnp.clip(offset[0] // (BLOCK * ROWS), 0, height // BLOCK - WINDOW)

    cut = lax.all_to_all(cut_tiles(reflectors.T), "row", split_axis=0, concat_axis=0, tiled=True)
    cut = cut.reshape(height // BLOCK, refl, BLOCK)
    skips = [sum(PARTS[:k]) for k in range(len(PARTS))]
    mine = lax.dynamic_slice_in_dim(cut, w0, WINDOW, 0)
    across = lax.ppermute(mine, "col", col_perm(1, 0))
    pairs = [jnp.stack([mine[k : k + n], across[k : k + n]]) for k, n in zip(skips, PARTS)]

    source = vectors.reshape(height // (ROWS * TILE), ROWS, TILE, width).transpose(1, 0, 2, 3)
    source, _ = lax.optimization_barrier((source, across))
    cyc_v = lax.all_to_all(source, "row", split_axis=0, concat_axis=0, tiled=True).reshape(height, width)

    infos, ids = {}, []
    for g in ORDER:
        base = ((zz + g) % 4) * refl
        starts = [(xl ^ half) * 4 * refl + base for half in range(2)]
        infos[g] = jnp.stack([w0, position, offset[0], band[0], *starts]).astype(jnp.int32)
        ids += [start + jnp.arange(refl) for start in starts]
    ids = jnp.concatenate(ids)
    t_rel = tmat[ids][:, ids]
    infos[0] = infos[0] + (t_rel[0, 0] * 0.0).astype(jnp.int32)

    ready = ()

    def arrive(k, g, halves):
        nonlocal ready
        *ready, done = prepare(infos[g], halves, ORDER.index(g), skips[k], height, nb, ready)
        return done

    def forward(up, down, done):
        zero = sum(token[0, 0] for token in done)
        far0 = lax.ppermute(up[:1] + zero, "col", col_perm(0, 1))
        far1 = lax.ppermute(down[1:] + zero, "col", col_perm(0, 3))
        return (far0, 0), (far1, 0)

    both = [
        (lax.ppermute(pair, "col", col_perm(0, 1)), lax.ppermute(pair, "col", col_perm(0, 3)))
        for pair in pairs
    ]
    done = [arrive(k, 0, ((pair, 0), (pair, 1))) for k, pair in enumerate(pairs)]
    fars = []
    for k, (up, down) in enumerate(both):
        fars.append(forward(up, down, done))
        done = [arrive(k, 1, ((down, 0), (down, 1))), arrive(k, 3, ((up, 0), (up, 1)))]
    info = w0[None].astype(jnp.int32)
    for k in range(len(PARTS)):
        arrive(k, 2, fars[k])
    high, low, high_t, low_t = ready
    partial_value = project(info, cyc_v, high, low)
    products = sum_over_rows(partial_value, position)
    return apply(info, cyc_v, t_rel, products, high_t, low_t)


def solution(mesh):
    placed = (P("row", "col"), P("row", "col"), P(), P(), P())
    return jax.shard_map(
        per_device, mesh=mesh, in_specs=placed, out_specs=P("row", "col"), check_vma=False
    )
```

```python
import functools

import jax
import jax.numpy as jnp
from jax import lax
from jax.experimental import pallas as pl
from jax.experimental.pallas import tpu as pltpu
from jax.sharding import PartitionSpec as P

TILE = 64
BLOCK = 2 * TILE
WINDOW = 50
SPAN = WINDOW * BLOCK
STEP = 5
PARTS = (30, 20)
ORDER = (0, 1, 3, 2)
ROWS = 16
F32, BF16 = jnp.float32, jnp.bfloat16
PARAMS = pltpu.CompilerParams(vmem_limit_bytes=60 * 2**20)


def col_perm(dl, dz):
    return [
        (low * 4 + z, (low ^ dl) * 4 + (z + dz) % 4) for low in range(2) for z in range(4)
    ]


def tile_kernel(y_ref, out_ref):
    lanes = lax.broadcasted_iota(jnp.int32, (y_ref.shape[0], BLOCK), 1)
    low = lanes < TILE
    for q in range(8):
        first = y_ref[:, q * BLOCK : (q + 1) * BLOCK]
        second = y_ref[:, 1024 + q * BLOCK : 1024 + (q + 1) * BLOCK]
        out_ref[2 * q, 0] = jnp.where(low, first, pltpu.roll(second, TILE, 1))
        out_ref[2 * q + 1, 0] = jnp.where(low, pltpu.roll(first, TILE, 1), second)


def cut_tiles(y_t):
    refl, height = y_t.shape
    steps = height // 2048
    return pl.pallas_call(
        tile_kernel,
        grid=(steps,),
        in_specs=[pl.BlockSpec((refl, 2048), lambda i: (0, i))],
        out_specs=pl.BlockSpec((ROWS, 1, refl, BLOCK), lambda i: (0, i, 0, 0)),
        out_shape=jax.ShapeDtypeStruct((ROWS, steps, refl, BLOCK), F32),
        name="cut_tiles",
        compiler_params=PARAMS,
    )(y_t)


def split(value):
    high = value.astype(BF16)
    return high, (value - high.astype(F32)).astype(BF16)


def prepare_kernel(skip, info, *refs):
    halves, (high, low, high_t, low_t, done) = refs[:2], refs[-5:]
    done[...] = jnp.zeros_like(done)
    rows = halves[0].shape[2]
    step = pl.program_id(0)
    lane = lax.broadcasted_iota(jnp.int32, (rows, BLOCK), 1)
    spread = (lane // TILE) * (ROWS * TILE) + lane % TILE
    spread = spread - lax.broadcasted_iota(jnp.int32, (rows, BLOCK), 0)
    band = info[3]
    for w in range(STEP):
        start = (info[0] + skip + step * STEP + w) * (BLOCK * ROWS) + info[1] * TILE - info[2]
        parts = []
        for half in range(2):
            away = spread + (start - info[4 + half])
            kept = jnp.where((away > 0) & (away < band), halves[half][0, w], 0.0)
            parts.append(jnp.where(away == 0, 1.0, kept))
        value = jnp.concatenate(parts, axis=0)
        at = slice(w * BLOCK, (w + 1) * BLOCK)
        high[:, at], low[:, at] = split(value)
        high_t[0, at, :], low_t[0, at, :] = split(value.T)


def prepare(info, halves, place, skip, height, count, before):
    arrays = [array for array, _ in halves]
    blocks, rows = arrays[0].shape[1:3]
    specs = [
        pl.BlockSpec((1, STEP, rows, BLOCK), functools.partial(lambda lead, i, s: (lead, i, 0, 0), lead))
        for _, lead in halves
    ]
    aliases = {3 + k: k for k in range(len(before))}
    specs += [pl.BlockSpec(memory_space=pl.ANY)] * len(before)
    wide = jax.ShapeDtypeStruct((count, SPAN), BF16)
    tall = jax.ShapeDtypeStruct((count // BLOCK, height, BLOCK), BF16)
    wide_spec = pl.BlockSpec((BLOCK, STEP * BLOCK), lambda i, s: (place, i + skip // STEP))
    tall_spec = pl.BlockSpec(
        (pl.Element(1), pl.Element(STEP * BLOCK), pl.Element(BLOCK)),
        lambda i, s: (place, pl.multiple_of((s[0] + skip + i * STEP) * BLOCK, BLOCK), 0),
    )
    done = jax.ShapeDtypeStruct((8, BLOCK), F32)
    done_spec = pl.BlockSpec((8, BLOCK), lambda i, s: (0, 0))
    return pl.pallas_call(
        functools.partial(prepare_kernel, skip),
        grid_spec=pltpu.PrefetchScalarGridSpec(
            num_scalar_prefetch=1,
            grid=(blocks // STEP,),
            in_specs=specs,
            out_specs=[wide_spec, wide_spec, tall_spec, tall_spec, done_spec],
        ),
        out_shape=[wide, wide, tall, tall, done],
        input_output_aliases=aliases,
        name="prepare",
        compiler_params=PARAMS,
        cost_estimate=pl.CostEstimate(flops=10**9, bytes_accessed=10**7, transcendentals=0),
    )(info, *arrays, *before)


def dot(a, b):
    return jnp.dot(a, b, preferred_element_type=F32)


def project_kernel(info, v_ref, high_ref, low_ref, out):
    @pl.when(pl.program_id(0) == 0)
    def _():
        out[...] = jnp.zeros_like(out)

    v_high, v_low = split(v_ref[...])
    high = high_ref[...]
    left = jnp.concatenate([high, low_ref[...], high], axis=1)
    out[...] += dot(left, jnp.concatenate([v_high, v_high, v_low], axis=0))


def project(info, cyc_v, high, low):
    width, count = cyc_v.shape[1], high.shape[0]
    rows = 2 * STEP * BLOCK
    wide = pl.BlockSpec((count, rows), lambda i, s: (0, i))
    window = pl.BlockSpec(
        (pl.Element(rows), pl.Element(width)),
        lambda i, s: (pl.multiple_of(s[0] * BLOCK + i * rows, BLOCK), 0),
    )
    return pl.pallas_call(
        project_kernel,
        grid_spec=pltpu.PrefetchScalarGridSpec(
            num_scalar_prefetch=1,
            grid=(SPAN // rows,),
            in_specs=[window, wide, wide],
            out_specs=pl.BlockSpec((count, width), lambda i, s: (0, 0)),
        ),
        out_shape=jax.ShapeDtypeStruct((count, width), F32),
        name="project",
        compiler_params=PARAMS,
        cost_estimate=pl.CostEstimate(flops=6 * count * SPAN * width, bytes_accessed=2 * 10**7, transcendentals=0),
    )(info, cyc_v, high, low)


def apply_kernel(info, v_ref, t_ref, p_ref, high_ref, low_ref, out, w_all):
    step = pl.program_id(0)
    rows = v_ref.shape[0]

    @pl.when(step == 0)
    def _():
        t_high, t_low = split(t_ref[...])
        p_high, p_low = split(p_ref[...])
        weights = dot(t_high, p_high) + dot(t_low, p_high) + dot(t_high, p_low)
        w_high, w_low = split(weights)
        w_all[...] = jnp.concatenate([w_high, w_high, w_low], axis=0)

    start = info[0] * BLOCK - step * rows
    touched = (start < rows) & (start + SPAN > 0)

    @pl.when(touched)
    def _():
        high = [high_ref[g] for g in range(4)]
        low = [low_ref[g] for g in range(4)]
        change = dot(jnp.concatenate(high + low + high, axis=1), w_all[...])
        at = lax.broadcasted_iota(jnp.int32, change.shape, 0) - start
        value = v_ref[...]
        out[...] = jnp.where((at >= 0) & (at < SPAN), value - change, value)

    @pl.when(jnp.logical_not(touched))
    def _():
        out[...] = v_ref[...]


def apply(info, cyc_v, t_rel, products, high, low):
    nb, (height, width) = high.shape[0] * BLOCK, cyc_v.shape
    rows = 8 * BLOCK
    held = lambda i, s: jnp.clip(i, s[0] * BLOCK // rows, (s[0] * BLOCK + SPAN - 1) // rows)
    tall = pl.BlockSpec((nb // BLOCK, rows, BLOCK), lambda i, s: (0, held(i, s), 0))
    plain = pl.BlockSpec((rows, width), lambda i, s: (i, 0))
    return pl.pallas_call(
        apply_kernel,
        grid_spec=pltpu.PrefetchScalarGridSpec(
            num_scalar_prefetch=1,
            grid=(height // rows,),
            in_specs=[
                plain,
                pl.BlockSpec((nb, nb), lambda i, s: (0, 0)),
                pl.BlockSpec((nb, width), lambda i, s: (0, 0)),
            ]
            + [tall] * 2,
            out_specs=plain,
            scratch_shapes=[pltpu.VMEM((3 * nb, width), BF16)],
        ),
        out_shape=jax.ShapeDtypeStruct(cyc_v.shape, F32),
        name="apply",
        compiler_params=PARAMS,
        cost_estimate=pl.CostEstimate(flops=6 * 512 * SPAN * 256, bytes_accessed=3 * 10**7, transcendentals=0),
    )(info, cyc_v, t_rel, products, high, low)


def row_perm(dx, dy, dc):
    return [
        (x * 8 + y * 2 + c, (x ^ dx) * 8 + ((y + dy) % 4) * 2 + (c ^ dc))
        for x in range(2)
        for y in range(4)
        for c in range(2)
    ]


def sum_over_rows(value, position):
    core_perm, x_perm = row_perm(0, 0, 1), row_perm(1, 0, 0)
    cc, xh = position % 2, position // 8

    def halve(value, bit, perm):
        n = value.shape[0] // 2
        keep = lax.dynamic_slice_in_dim(value, bit * n, n, 0)
        give = lax.dynamic_slice_in_dim(value, (1 - bit) * n, n, 0)
        return keep + lax.ppermute(give, "row", perm)

    def join(value, bit, perm):
        other = lax.ppermute(value, "row", perm)
        first, second = jnp.where(bit == 0, value, other), jnp.where(bit == 0, other, value)
        return jnp.concatenate([first, second])

    value = halve(halve(value, cc, core_perm), xh, x_perm)
    for flip in (1, 3):
        pairs = [(r, r ^ (2 * flip)) for r in range(16)]
        value = value + lax.ppermute(value, "row", pairs)
    return join(join(value, xh, x_perm), cc, core_perm)


def per_device(vectors, reflectors, tmat, offset, band):
    height, width = vectors.shape
    refl = reflectors.shape[1]
    nb = 8 * refl
    position = lax.axis_index("row")
    place = lax.axis_index("col")
    xl, zz = place // 4, place % 4
    w0 = jnp.clip(offset[0] // (BLOCK * ROWS), 0, height // BLOCK - WINDOW)

    cut = lax.all_to_all(cut_tiles(reflectors.T), "row", split_axis=0, concat_axis=0, tiled=True)
    cut = cut.reshape(height // BLOCK, refl, BLOCK)
    skips = [sum(PARTS[:k]) for k in range(len(PARTS))]
    mine = lax.dynamic_slice_in_dim(cut, w0, WINDOW, 0)
    across = lax.ppermute(mine, "col", col_perm(1, 0))
    pairs = [jnp.stack([mine[k : k + n], across[k : k + n]]) for k, n in zip(skips, PARTS)]

    source = vectors.reshape(height // (ROWS * TILE), ROWS, TILE, width).transpose(1, 0, 2, 3)
    source, _ = lax.optimization_barrier((source, across))
    cyc_v = lax.all_to_all(source, "row", split_axis=0, concat_axis=0, tiled=True).reshape(height, width)

    infos, ids = {}, []
    for g in ORDER:
        base = ((zz + g) % 4) * refl
        starts = [(xl ^ half) * 4 * refl + base for half in range(2)]
        infos[g] = jnp.stack([w0, position, offset[0], band[0], *starts]).astype(jnp.int32)
        ids += [start + jnp.arange(refl) for start in starts]
    ids = jnp.concatenate(ids)
    t_rel = tmat[ids][:, ids]
    infos[0] = infos[0] + (t_rel[0, 0] * 0.0).astype(jnp.int32)

    ready = ()

    def arrive(k, g, halves):
        nonlocal ready
        *ready, done = prepare(infos[g], halves, ORDER.index(g), skips[k], height, nb, ready)
        return done

    def forward(up, down, done):
        zero = sum(token[0, 0] for token in done)
        far0 = lax.ppermute(up[:1] + zero, "col", col_perm(0, 1))
        far1 = lax.ppermute(down[1:] + zero, "col", col_perm(0, 3))
        return (far0, 0), (far1, 0)

    both = [
        (lax.ppermute(pair, "col", col_perm(0, 1)), lax.ppermute(pair, "col", col_perm(0, 3)))
        for pair in pairs
    ]
    done = [arrive(k, 0, ((pair, 0), (pair, 1))) for k, pair in enumerate(pairs)]
    fars = []
    for k, (up, down) in enumerate(both):
        fars.append(forward(up, down, done))
        done = [arrive(k, 1, ((down, 0), (down, 1))), arrive(k, 3, ((up, 0), (up, 1)))]
    info = w0[None].astype(jnp.int32)
    for k in range(len(PARTS)):
        arrive(k, 2, fars[k])
    high, low, high_t, low_t = ready
    partial_value = project(info, cyc_v, high, low)
    products = sum_over_rows(partial_value, position)
    return apply(info, cyc_v, t_rel, products, high_t, low_t)


def solution(mesh):
    placed = (P("row", "col"), P("row", "col"), P(), P(), P())
    return jax.shard_map(
        per_device, mesh=mesh, in_specs=placed, out_specs=P("row", "col"), check_vma=False
    )
```

```python
import functools

import jax
import jax.numpy as jnp
from jax import lax
from jax.experimental import pallas as pl
from jax.experimental.pallas import tpu as pltpu
from jax.sharding import PartitionSpec as P

TILE = 64
BLOCK = 2 * TILE
WINDOW = 50
SPAN = WINDOW * BLOCK
STEP = 5
PARTS = (30, 20)
ORDER = (0, 1, 3, 2)
ROWS = 16
F32, BF16 = jnp.float32, jnp.bfloat16
PARAMS = pltpu.CompilerParams(vmem_limit_bytes=60 * 2**20)


def col_perm(dl, dz):
    return [
        (low * 4 + z, (low ^ dl) * 4 + (z + dz) % 4) for low in range(2) for z in range(4)
    ]


def tile_kernel(y_ref, out_ref):
    lanes = lax.broadcasted_iota(jnp.int32, (y_ref.shape[0], BLOCK), 1)
    low = lanes < TILE
    for q in range(8):
        first = y_ref[:, q * BLOCK : (q + 1) * BLOCK]
        second = y_ref[:, 1024 + q * BLOCK : 1024 + (q + 1) * BLOCK]
        out_ref[2 * q, 0] = jnp.where(low, first, pltpu.roll(second, TILE, 1))
        out_ref[2 * q + 1, 0] = jnp.where(low, pltpu.roll(first, TILE, 1), second)


def cut_tiles(y_t):
    refl, height = y_t.shape
    steps = height // 2048
    return pl.pallas_call(
        tile_kernel,
        grid=(steps,),
        in_specs=[pl.BlockSpec((refl, 2048), lambda i: (0, i))],
        out_specs=pl.BlockSpec((ROWS, 1, refl, BLOCK), lambda i: (0, i, 0, 0)),
        out_shape=jax.ShapeDtypeStruct((ROWS, steps, refl, BLOCK), F32),
        name="cut_tiles",
        compiler_params=PARAMS,
    )(y_t)


def split(value):
    high = value.astype(BF16)
    return high, (value - high.astype(F32)).astype(BF16)


def prepare_kernel(skip, info, *refs):
    halves, (high, low, high_t, low_t, done) = refs[:2], refs[-5:]
    done[...] = jnp.zeros_like(done)
    rows = halves[0].shape[2]
    step = pl.program_id(0)
    lane = lax.broadcasted_iota(jnp.int32, (rows, BLOCK), 1)
    spread = (lane // TILE) * (ROWS * TILE) + lane % TILE
    spread = spread - lax.broadcasted_iota(jnp.int32, (rows, BLOCK), 0)
    band = info[3]
    for w in range(STEP):
        start = (info[0] + skip + step * STEP + w) * (BLOCK * ROWS) + info[1] * TILE - info[2]
        parts = []
        for half in range(2):
            away = spread + (start - info[4 + half])
            kept = jnp.where((away > 0) & (away < band), halves[half][0, w], 0.0)
            parts.append(jnp.where(away == 0, 1.0, kept))
        value = jnp.concatenate(parts, axis=0)
        at = slice(w * BLOCK, (w + 1) * BLOCK)
        high[:, at], low[:, at] = split(value)
        high_t[0, at, :], low_t[0, at, :] = split(value.T)


def prepare(info, halves, place, skip, height, count, before):
    arrays = [array for array, _ in halves]
    blocks, rows = arrays[0].shape[1:3]
    specs = [
        pl.BlockSpec((1, STEP, rows, BLOCK), functools.partial(lambda lead, i, s: (lead, i, 0, 0), lead))
        for _, lead in halves
    ]
    aliases = {3 + k: k for k in range(len(before))}
    specs += [pl.BlockSpec(memory_space=pl.ANY)] * len(before)
    wide = jax.ShapeDtypeStruct((count, SPAN), BF16)
    tall = jax.ShapeDtypeStruct((count // BLOCK, height, BLOCK), BF16)
    wide_spec = pl.BlockSpec((BLOCK, STEP * BLOCK), lambda i, s: (place, i + skip // STEP))
    tall_spec = pl.BlockSpec(
        (pl.Element(1), pl.Element(STEP * BLOCK), pl.Element(BLOCK)),
        lambda i, s: (place, pl.multiple_of((s[0] + skip + i * STEP) * BLOCK, BLOCK), 0),
    )
    done = jax.ShapeDtypeStruct((8, BLOCK), F32)
    done_spec = pl.BlockSpec((8, BLOCK), lambda i, s: (0, 0))
    return pl.pallas_call(
        functools.partial(prepare_kernel, skip),
        grid_spec=pltpu.PrefetchScalarGridSpec(
            num_scalar_prefetch=1,
            grid=(blocks // STEP,),
            in_specs=specs,
            out_specs=[wide_spec, wide_spec, tall_spec, tall_spec, done_spec],
        ),
        out_shape=[wide, wide, tall, tall, done],
        input_output_aliases=aliases,
        name="prepare",
        compiler_params=PARAMS,
        cost_estimate=pl.CostEstimate(flops=10**9, bytes_accessed=10**7, transcendentals=0),
    )(info, *arrays, *before)


def dot(a, b):
    return jnp.dot(a, b, preferred_element_type=F32)


def project_kernel(info, v_ref, high_ref, low_ref, out):
    @pl.when(pl.program_id(0) == 0)
    def _():
        out[...] = jnp.zeros_like(out)

    v_high, v_low = split(v_ref[...])
    high = high_ref[...]
    left = jnp.concatenate([high, low_ref[...], high], axis=1)
    out[...] += dot(left, jnp.concatenate([v_high, v_high, v_low], axis=0))


def project(info, cyc_v, high, low):
    width, count = cyc_v.shape[1], high.shape[0]
    rows = 5 * STEP * BLOCK
    wide = pl.BlockSpec((count, rows), lambda i, s: (0, i))
    window = pl.BlockSpec(
        (pl.Element(rows), pl.Element(width)),
        lambda i, s: (pl.multiple_of(s[0] * BLOCK + i * rows, BLOCK), 0),
    )
    return pl.pallas_call(
        project_kernel,
        grid_spec=pltpu.PrefetchScalarGridSpec(
            num_scalar_prefetch=1,
            grid=(SPAN // rows,),
            in_specs=[window, wide, wide],
            out_specs=pl.BlockSpec((count, width), lambda i, s: (0, 0)),
        ),
        out_shape=jax.ShapeDtypeStruct((count, width), F32),
        name="project",
        compiler_params=PARAMS,
        cost_estimate=pl.CostEstimate(flops=6 * count * SPAN * width, bytes_accessed=2 * 10**7, transcendentals=0),
    )(info, cyc_v, high, low)


def apply_kernel(info, v_ref, t_ref, p_ref, high_ref, low_ref, out, w_all):
    step = pl.program_id(0)
    rows = v_ref.shape[0]

    @pl.when(step == 0)
    def _():
        t_high, t_low = split(t_ref[...])
        p_high, p_low = split(p_ref[...])
        weights = dot(t_high, p_high) + dot(t_low, p_high) + dot(t_high, p_low)
        w_high, w_low = split(weights)
        w_all[...] = jnp.concatenate([w_high, w_high, w_low], axis=0)

    start = info[0] * BLOCK - step * rows
    touched = (start < rows) & (start + SPAN > 0)

    @pl.when(touched)
    def _():
        high = [high_ref[g] for g in range(4)]
        low = [low_ref[g] for g in range(4)]
        change = dot(jnp.concatenate(high + low + high, axis=1), w_all[...])
        at = lax.broadcasted_iota(jnp.int32, change.shape, 0) - start
        value = v_ref[...]
        out[...] = jnp.where((at >= 0) & (at < SPAN), value - change, value)

    @pl.when(jnp.logical_not(touched))
    def _():
        out[...] = v_ref[...]


def apply(info, cyc_v, t_rel, products, high, low):
    nb, (height, width) = high.shape[0] * BLOCK, cyc_v.shape
    rows = 16 * BLOCK
    held = lambda i, s: jnp.clip(i, s[0] * BLOCK // rows, (s[0] * BLOCK + SPAN - 1) // rows)
    tall = pl.BlockSpec((nb // BLOCK, rows, BLOCK), lambda i, s: (0, held(i, s), 0))
    plain = pl.BlockSpec((rows, width), lambda i, s: (i, 0))
    return pl.pallas_call(
        apply_kernel,
        grid_spec=pltpu.PrefetchScalarGridSpec(
            num_scalar_prefetch=1,
            grid=(height // rows,),
            in_specs=[
                plain,
                pl.BlockSpec((nb, nb), lambda i, s: (0, 0)),
                pl.BlockSpec((nb, width), lambda i, s: (0, 0)),
            ]
            + [tall] * 2,
            out_specs=plain,
            scratch_shapes=[pltpu.VMEM((3 * nb, width), BF16)],
        ),
        out_shape=jax.ShapeDtypeStruct(cyc_v.shape, F32),
        name="apply",
        compiler_params=PARAMS,
        cost_estimate=pl.CostEstimate(flops=6 * 512 * SPAN * 256, bytes_accessed=3 * 10**7, transcendentals=0),
    )(info, cyc_v, t_rel, products, high, low)


def row_perm(dx, dy, dc):
    return [
        (x * 8 + y * 2 + c, (x ^ dx) * 8 + ((y + dy) % 4) * 2 + (c ^ dc))
        for x in range(2)
        for y in range(4)
        for c in range(2)
    ]


def sum_over_rows(value, position):
    core_perm, x_perm = row_perm(0, 0, 1), row_perm(1, 0, 0)
    cc, xh = position % 2, position // 8

    def halve(value, bit, perm):
        n = value.shape[0] // 2
        keep = lax.dynamic_slice_in_dim(value, bit * n, n, 0)
        give = lax.dynamic_slice_in_dim(value, (1 - bit) * n, n, 0)
        return keep + lax.ppermute(give, "row", perm)

    def join(value, bit, perm):
        other = lax.ppermute(value, "row", perm)
        first, second = jnp.where(bit == 0, value, other), jnp.where(bit == 0, other, value)
        return jnp.concatenate([first, second])

    value = halve(halve(value, cc, core_perm), xh, x_perm)
    value = value + sum(lax.ppermute(value, "row", row_perm(0, dy, 0)) for dy in (1, 2, 3))
    return join(join(value, xh, x_perm), cc, core_perm)


def per_device(vectors, reflectors, tmat, offset, band):
    height, width = vectors.shape
    refl = reflectors.shape[1]
    nb = 8 * refl
    position = lax.axis_index("row")
    place = lax.axis_index("col")
    xl, zz = place // 4, place % 4
    w0 = jnp.clip(offset[0] // (BLOCK * ROWS), 0, height // BLOCK - WINDOW)

    cut = lax.all_to_all(cut_tiles(reflectors.T), "row", split_axis=0, concat_axis=0, tiled=True)
    cut = cut.reshape(height // BLOCK, refl, BLOCK)
    skips = [sum(PARTS[:k]) for k in range(len(PARTS))]
    mine = lax.dynamic_slice_in_dim(cut, w0, WINDOW, 0)
    across = lax.ppermute(mine, "col", col_perm(1, 0))
    pairs = [jnp.stack([mine[k : k + n], across[k : k + n]]) for k, n in zip(skips, PARTS)]

    source = vectors.reshape(height // (ROWS * TILE), ROWS, TILE, width).transpose(1, 0, 2, 3)
    source, _ = lax.optimization_barrier((source, across))
    cyc_v = lax.all_to_all(source, "row", split_axis=0, concat_axis=0, tiled=True).reshape(height, width)

    infos, ids = {}, []
    for g in ORDER:
        base = ((zz + g) % 4) * refl
        starts = [(xl ^ half) * 4 * refl + base for half in range(2)]
        infos[g] = jnp.stack([w0, position, offset[0], band[0], *starts]).astype(jnp.int32)
        ids += [start + jnp.arange(refl) for start in starts]
    ids = jnp.concatenate(ids)
    t_rel = tmat[ids][:, ids]
    infos[0] = infos[0] + (t_rel[0, 0] * 0.0).astype(jnp.int32)

    ready = ()

    def arrive(k, g, halves):
        nonlocal ready
        *ready, done = prepare(infos[g], halves, ORDER.index(g), skips[k], height, nb, ready)
        return done

    def forward(up, down, done):
        zero = sum(token[0, 0] for token in done)
        far0 = lax.ppermute(up[:1] + zero, "col", col_perm(0, 1))
        far1 = lax.ppermute(down[1:] + zero, "col", col_perm(0, 3))
        return (far0, 0), (far1, 0)

    both = [
        (lax.ppermute(pair, "col", col_perm(0, 1)), lax.ppermute(pair, "col", col_perm(0, 3)))
        for pair in pairs
    ]
    done = [arrive(k, 0, ((pair, 0), (pair, 1))) for k, pair in enumerate(pairs)]
    fars = []
    for k, (up, down) in enumerate(both):
        fars.append(forward(up, down, done))
        done = [arrive(k, 1, ((down, 0), (down, 1))), arrive(k, 3, ((up, 0), (up, 1)))]
    info = w0[None].astype(jnp.int32)
    for k in range(len(PARTS)):
        arrive(k, 2, fars[k])
    high, low, high_t, low_t = ready
    partial_value = project(info, cyc_v, high, low)
    products = sum_over_rows(partial_value, position)
    return apply(info, cyc_v, t_rel, products, high_t, low_t)


def solution(mesh):
    placed = (P("row", "col"), P("row", "col"), P(), P(), P())
    return jax.shard_map(
        per_device, mesh=mesh, in_specs=placed, out_specs=P("row", "col"), check_vma=False
    )
```
